32 devices in a mesh: los: 4 (over y, x), sky: 8 (over z, core).
Axes of the slice: x: 2, y: 2, z: 4, core: 2. Of those that a mesh axis runs over, the one named last changes fastest.
Arguments:
- state: float32 [12, 32768], P(None, ('los', 'sky')), may hold values from -6 to 6
- deflection: bfloat16 [4, 2, 64, 2048], P('los', None, None, 'sky'), may hold values from -6 to 6
- shear: bfloat16 [4, 2, 96, 2048], P('los', None, None, 'sky'), may hold values from -3 to 3
- routes: int32 [4, 2, 32768, 1], P(None, None, ('los', 'sky')), may hold values from 0 to 7; in each aligned block of 1024 rows (0 to 1023, 1024 to 2047, ..., all dimensions but the last counted through in order) at most 256 rows name the same one
- patches: int32 [4, 2, 32768], P(None, None, ('los', 'sky')), may hold values from 0 to 255
Outputs:
- traced: float32 [12, 32768], P(None, ('los', 'sky'))
The draws below stay inside these ranges and needn't reach their ends.
Inputs may be any that keep to these rules, and one draw needn't show every extreme that they name: `routes`: in each hop and plane, one device's 1024 slots name one tile at most 256 times, and exactly 256 times in some.
All inputs are finite; a program needn't handle non-finite values.
Results may differ from the reference program's by a relative error of at most 0.0003.
Values sent between devices are 32-bit elements; how exact they have to be, the bound alone decides.
A program may use at most 64 MiB of HBM per device.

```python
import math
import jax
import jax.numpy as jnp
import numpy as np
from jax import lax

RAYS_DEV = 1024
PATCHES = 256
HOPS = 4
CAP = 256
TOTAL_RAYS = 32768
N_LOS = 4
N_SKY = 8


def with_ends(entries, own_key, least, largest):
    place = [jax.random.randint(jax.random.fold_in(own_key, axis), (), 0, length) for axis, length in enumerate(entries.shape)]
    main_axis = entries.shape.index(max(entries.shape))
    beside = place[:main_axis] + [(place[main_axis] + 1) % entries.shape[main_axis]] + place[main_axis + 1:]
    return entries.at[tuple(place)].set(least).at[tuple(beside)].set(largest)


def steps_of(own_key, shape, cuts, least, largest):
    def one(position, shards_of):
        steps = jax.random.uniform(jax.random.fold_in(jax.random.fold_in(own_key, 6), position), (shards_of,), jnp.float32, least / len(cuts), largest / len(cuts))
        return jnp.repeat(jnp.exp(steps), shape[position] // shards_of).reshape((-1,) + (1,) * (len(shape) - position - 1))

    level = one(*cuts[0])
    for cut in cuts[1:]:
        level = level * one(*cut)
    return level


def shared_out(rng, own, number, rows, amount, top, bound, slope):
    order = jax.random.permutation(rng, amount)
    heavy_load, ordinary = portions_of(amount, rows * top, bound, slope, True), portions_of(amount, rows * top, bound, slope, False)
    places = jnp.arange(amount)

    def named(tallies, turn):
        used = int((tallies > 0).sum())
        fixed = max(1, used // 4)
        passed = fixed + (places - fixed + turn * (used - fixed)) % max(1, amount - fixed)
        return jnp.zeros((amount,), jnp.int32).at[order[jnp.where(places < fixed, places, passed)]].set(jnp.asarray(tallies, jnp.int32))

    tallies = jnp.where(number % 4 == 0, named(heavy_load, number // 4), named(ordinary, number - number // 4 - 1))
    mixed = jax.random.permutation(jax.random.fold_in(own, 3), amount)
    source_of, receiver = mixed[0:amount // 2 * 2:2], mixed[1:amount // 2 * 2:2]
    room = jnp.minimum(tallies[source_of] - 1, bound - tallies[receiver]) // 2
    room = jnp.where((source_of == order[0]) | (receiver == order[0]) | (tallies[receiver] == 0), 0, jnp.maximum(room, 0))
    passed = jax.random.randint(jax.random.fold_in(own, 4), (amount // 2,), 0, 1 << 20) % (room + 1)
    tallies = tallies.at[source_of].add(-passed).at[receiver].add(passed)
    items = jnp.searchsorted(jnp.cumsum(tallies), jnp.arange(rows * top), side="right").astype(jnp.int32)
    listing = items.reshape(top, rows).T
    listing = listing[jax.random.permutation(jax.random.fold_in(own, 1), rows)]
    turn = jax.random.randint(jax.random.fold_in(own, 2), (rows, 1), 0, top)
    return jnp.take_along_axis(listing, (jnp.arange(top)[None, :] + turn) % top, axis=1)


def portions_of(amount, total, most, lean, full):
    weights = [(1 << 20) // math.isqrt(rank ** lean) + 1 for rank in range(1, amount + 1)]
    largest = most if full else min(most, max(-(-total // amount), total * weights[0] // sum(weights)))
    least = 1 if total - largest >= amount - 1 else 0
    counts, rest = [largest] + [least] * (amount - 1), total - largest - least * (amount - 1)
    while rest > 0:
        movable = [i for i in range(1, amount) if counts[i] < largest] or [i for i in range(1, amount) if counts[i] < most]
        pool, remaining = sum([weights[i] for i in movable]), rest
        for i in movable:
            extra = min(most - counts[i], max(1, remaining * weights[i] // pool), rest)
            counts[i] = counts[i] + extra
            rest = rest - extra
    return np.array(counts)


def noise(rng, dims, width, most, cuts=(), kind=jnp.bfloat16):
    factor_of = steps_of(rng, dims, cuts, -0.22, 0.18) if cuts else 1.0
    values = jax.random.normal(rng, dims, jnp.float32) * width * factor_of
    return jnp.minimum(jnp.maximum(values, -most), most).astype(kind)


def setup_inputs(seed: int = 0) -> dict:
    splits = jax.random.split(jax.random.key(seed), 6)
    state = noise(splits[0], (12, TOTAL_RAYS), 1.0, 6.0, ((1, 32),), jnp.float32)
    deflection = noise(splits[1], (N_LOS, 2, 64, N_SKY * PATCHES), 1.0, 6.0, ((0, 4), (3, 8)))
    shear = noise(splits[2], (N_LOS, 2, 96, N_SKY * PATCHES), 0.5, 3.0, ((0, 4), (3, 8)))
    routes_keys = jax.random.split(jax.random.fold_in(splits[3], 1), HOPS * 2 * TOTAL_RAYS // RAYS_DEV)
    routes_turns = jax.random.permutation(jax.random.fold_in(splits[3], 3), HOPS * 2 * TOTAL_RAYS // RAYS_DEV)
    routes = jax.vmap(lambda own, number: shared_out(jax.random.fold_in(splits[3], 2), own, number, RAYS_DEV, N_SKY, 1, CAP, 2))(routes_keys, routes_turns).reshape((HOPS, 2, TOTAL_RAYS, 1))
    patches = with_ends(jax.random.randint(splits[4], (HOPS, 2, TOTAL_RAYS), 0, PATCHES), jax.random.fold_in(splits[4], 1), 0, PATCHES - 1).astype(jnp.int32)
    return dict(state=state, deflection=deflection, shear=shear, routes=routes, patches=patches)


def weights(pos_x, pos_y):
    across = jnp.arange(4).astype(pos_x.dtype)
    along = jnp.arange(8).astype(pos_x.dtype)
    kern_x = (1.0 + jnp.cos(2.0 * math.pi * (pos_x[None, :] - across[:, None]) / 4.0)) / 4.0
    kern_y = (1.0 + jnp.cos(2.0 * math.pi * (pos_y[None, :] - along[:, None]) / 8.0)) / 8.0
    return (kern_x[:, None, :] * kern_y[None, :, :]).reshape(32, -1)


def interpolate(raw, pos_x, pos_y):
    table = weights(pos_x, pos_y)
    return jnp.sum(raw.reshape(5, 32, -1) * table[None], axis=1)


def advance(current, values):
    pos_x, pos_y, ang_x, ang_y, a11, a12, a21, a22, b11, b12, b21, b22 = [current[k] for k in range(12)]
    alpha_x, alpha_y, psi11, psi12, psi22 = [values[k] for k in range(5)]
    ang_x = ang_x - alpha_x
    ang_y = ang_y - alpha_y
    b11 = b11 - (psi11 * a11 + psi12 * a21)
    b12 = b12 - (psi11 * a12 + psi12 * a22)
    b21 = b21 - (psi12 * a11 + psi22 * a21)
    b22 = b22 - (psi12 * a12 + psi22 * a22)
    pos_x = pos_x + 0.5 * ang_x
    pos_y = pos_y + 0.5 * ang_y
    a11 = a11 + 0.5 * b11
    a12 = a12 + 0.5 * b12
    a21 = a21 + 0.5 * b21
    a22 = a22 + 0.5 * b22
    return jnp.stack([pos_x, pos_y, ang_x, ang_y, a11, a12, a21, a22, b11, b12, b21, b22])


def reference(state, deflection, shear, routes, patches):
    slab_rays = N_SKY * RAYS_DEV
    current = state.reshape(12, N_LOS, slab_rays).transpose(1, 0, 2)
    for hop in range(HOPS):
        for plane in range(2):
            dest = routes[hop, plane, :, 0].reshape(N_LOS, slab_rays)
            which = patches[hop, plane].reshape(N_LOS, slab_rays)

            def one_slab(items, plane=plane):
                rays, defl, shr, tile, patch = items
                fields = jnp.concatenate([defl[plane], shr[plane]], axis=0).astype(jnp.float32)
                column = (tile * PATCHES + patch).astype(jnp.int32)
                raw = jnp.take(fields, column, axis=1)
                return advance(rays, interpolate(raw, rays[0], rays[1]))

            current = lax.map(one_slab, (current, deflection, shear, dest, which))
        current = jnp.roll(current, 1, axis=0)
    return current.transpose(1, 0, 2).reshape(12, -1)
```

```python
import functools
import math

import jax
import jax.numpy as jnp
import ml_dtypes
import numpy as np
from jax import lax
from jax.experimental import pallas as pl
from jax.experimental.pallas import tpu as pltpu
from jax.sharding import PartitionSpec as P

MESH = pl.DeviceIdType.MESH
NX, NY, COMPS = 4, 8, 5
CELLS = NX * NY
BASIS = 9
SENT = 48
WIDE = BASIS * 8


def reduction():
    i, j = np.arange(NX), np.arange(NY)
    along_x = np.stack([np.ones(NX), np.cos(2 * math.pi * i / NX), np.sin(2 * math.pi * i / NX)])
    along_y = np.stack([np.ones(NY), np.cos(2 * math.pi * j / NY), np.sin(2 * math.pi * j / NY)])
    cells = np.einsum("ai,bj->abij", along_x, along_y).reshape(BASIS, CELLS) / CELLS
    cells[np.abs(cells) < 1e-12] = 0.0
    whole = np.zeros((SENT, COMPS * CELLS))
    for ab in range(BASIS):
        for k in range(COMPS):
            whole[ab * COMPS + k, k * CELLS:(k + 1) * CELLS] = cells[ab]
    pieces, rest = [], whole
    for _ in range(3):
        piece = rest.astype(ml_dtypes.bfloat16)
        pieces.append(piece)
        rest = rest - piece.astype(np.float64)
    return np.concatenate(pieces)


def cos_turns(turns):
    folded = turns - jnp.floor(turns + 0.5)
    z = (0.25 - jnp.abs(folded)) * (2.0 * math.pi)
    q = z * z
    series = jnp.full_like(q, -1.0 / 39916800.0)
    for term in (1.0 / 362880.0, -1.0 / 5040.0, 1.0 / 120.0, -1.0 / 6.0, 1.0):
        series = series * q + term
    return series * z


def advance(pos, vel, table):
    x, y = pos[0:1] * (1.0 / NX), pos[1:2] * (1.0 / NY)
    wave = cos_turns(jnp.concatenate([x, x - 0.25, y, y - 0.25], axis=0))
    cx, sx, cy, sy = [wave[k:k + 1] for k in range(4)]
    part = [table[ab * 8:(ab + 1) * 8] for ab in range(BASIS)]
    lines = [part[3 * a] + cy * part[3 * a + 1] + sy * part[3 * a + 2] for a in range(3)]
    vals = lines[0] + cx * lines[1] + sx * lines[2]
    p11, p12, p22 = vals[2:3], vals[3:4], vals[4:5]
    top, low = pos[2:4], pos[4:6]
    turn = jnp.concatenate([vals[0:2], p11 * top + p12 * low, p12 * top + p22 * low], axis=0)
    vel = vel - turn
    return pos + 0.5 * vel, vel


def kernel(
    n_los, tiles, hops,
    state_ref, defl_ref, shear_ref, routes_ref, patches_ref, reduce_ref, out_ref,
    gathered, tables, looked, outgoing, landed,
    send_sem, recv_sem, pass_sem, move_sem, land_sem,
):
    los, sky = lax.axis_index("los"), lax.axis_index("sky")
    rays, cells = state_ref.shape[1], defl_ref.shape[3]
    pair = sky + 1 - 2 * lax.rem(sky, 2)
    peers = [lax.rem(sky + 2 * step, tiles) for step in range(1, tiles // 2)]
    after, before = lax.rem(los + 1, n_los), lax.rem(los + n_los - 1, n_los)

    barrier = pltpu.get_barrier_semaphore()
    friends = [(los, peer) for peer in peers] + [(los, pair), (after, sky), (before, sky)]
    for friend in friends:
        pl.semaphore_signal(barrier, inc=1, device_id=friend, device_id_type=MESH)

    cut = defl_ref.shape[2]
    for plane in range(2):
        found = jnp.dot(reduce_ref[:, :cut], defl_ref[0, plane], preferred_element_type=jnp.float32)
        found += jnp.dot(reduce_ref[:, cut:], shear_ref[0, plane], preferred_element_type=jnp.float32)
        gathered[plane, sky] = found[:SENT] + (found[SENT:2 * SENT] + found[2 * SENT:])
    pl.semaphore_wait(barrier, len(friends))

    def sending(plane, tile, to, sent):
        return pltpu.make_async_remote_copy(
            src_ref=gathered.at[plane, tile], dst_ref=gathered.at[plane, tile],
            send_sem=sent, recv_sem=recv_sem.at[plane, tile],
            device_id=(los, to), device_id_type=MESH,
        )

    started = []
    for plane in range(2):
        for step, to in enumerate(peers + [pair]):
            copy = sending(plane, sky, to, send_sem.at[plane, step])
            copy.start()
            started.append(copy)

    def build(plane, tile):
        wide = jnp.concatenate(
            [gathered[plane, tile, ab * COMPS:ab * COMPS + 8, :] for ab in range(BASIS)], axis=0
        )
        high = wide.astype(jnp.bfloat16).astype(jnp.float32)
        tables[plane, tile] = jnp.concatenate([high, wide - high], axis=0).astype(jnp.bfloat16)

    def arrive(plane):
        build(plane, sky)
        for step, peer in enumerate(peers):
            sending(plane, peer, pair, pass_sem.at[plane, step]).wait_recv()
            copy = sending(plane, peer, pair, pass_sem.at[plane, step])
            copy.start()
            started.append(copy)
            build(plane, peer)
        for other in [pair] + [lax.rem(pair + 2 * step, tiles) for step in range(1, tiles // 2)]:
            sending(plane, other, pair, pass_sem.at[plane, 0]).wait_recv()
            build(plane, other)

    group = min(tiles, 8)

    def lookup(hop, plane):
        patch = patches_ref[hop, plane:plane + 1, :]
        route = jnp.broadcast_to(routes_ref[hop, plane:plane + 1, :], (8, rays))
        place = lax.broadcasted_iota(jnp.int32, (cells, rays), 0)
        onehot = jnp.where(place == patch, 1.0, 0.0).astype(jnp.bfloat16)
        chosen = None
        for first in range(0, tiles, group):
            rows = tables[plane, first:first + group].reshape(group * 2 * WIDE, cells)
            raw = jnp.dot(rows, onehot, preferred_element_type=jnp.float32)
            raw = raw.reshape(group, 2, BASIS, 8, rays)
            for tile in range(group):
                both = raw[tile, 0] + raw[tile, 1]
                named = jnp.broadcast_to(route[None], both.shape) == first + tile
                chosen = both if chosen is None else jnp.where(named, both, chosen)
        looked[lax.rem(hop, 2) if not isinstance(hop, int) else hop % 2, plane] = chosen.reshape(WIDE, rays)

    state = state_ref[...]
    pos = jnp.concatenate([state[0:2], state[4:8]], axis=0)
    vel = jnp.concatenate([state[2:4], state[8:12]], axis=0)
    moves = []
    for hop in range(hops):
        for plane in range(2):
            if hop == 0:
                arrive(plane)
                lookup(hop, plane)
            pos, vel = advance(pos, vel, looked[hop % 2, plane])
        outgoing[hop, 0:2] = pos[0:2]
        outgoing[hop, 2:4] = vel[0:2]
        outgoing[hop, 4:8] = pos[2:6]
        outgoing[hop, 8:12] = vel[2:6]
        move = pltpu.make_async_remote_copy(
            src_ref=outgoing.at[hop], dst_ref=landed.at[hop],
            send_sem=move_sem.at[hop], recv_sem=land_sem.at[hop],
            device_id=(after, sky), device_id_type=MESH,
        )
        move.start()
        moves.append(move)
        if hop + 1 < hops:
            lookup(hop + 1, 0)
            lookup(hop + 1, 1)
        move.wait_recv()
        if hop + 1 < hops:
            state = landed[hop]
            pos = jnp.concatenate([state[0:2], state[4:8]], axis=0)
            vel = jnp.concatenate([state[2:4], state[8:12]], axis=0)
    out_ref[...] = landed[hops - 1]
    for copy in started + moves:
        copy.wait_send()


def body(n_los, tiles, state, deflection, shear, routes, patches):
    hops, rays, cells = routes.shape[0], state.shape[1], deflection.shape[3]
    routes = routes.reshape(patches.shape)
    vmem = pl.BlockSpec(memory_space=pltpu.VMEM)
    return pl.pallas_call(
        functools.partial(kernel, n_los, tiles, hops),
        out_shape=jax.ShapeDtypeStruct(state.shape, jnp.float32),
        in_specs=[vmem] * 6,
        out_specs=vmem,
        scratch_shapes=[
            pltpu.VMEM((2, tiles, SENT, cells), jnp.float32),
            pltpu.VMEM((2, tiles, 2 * WIDE, cells), jnp.bfloat16),
            pltpu.VMEM((2, 2, WIDE, rays), jnp.float32),
            pltpu.VMEM((hops,) + state.shape, jnp.float32),
            pltpu.VMEM((hops,) + state.shape, jnp.float32),
            pltpu.SemaphoreType.DMA((2, tiles // 2)),
            pltpu.SemaphoreType.DMA((2, tiles)),
            pltpu.SemaphoreType.DMA((2, tiles // 2)),
            pltpu.SemaphoreType.DMA((hops,)),
            pltpu.SemaphoreType.DMA((hops,)),
        ],
        compiler_params=pltpu.CompilerParams(
            collective_id=0, has_side_effects=True, vmem_limit_bytes=48 * 2**20
        ),
    )(state, deflection, shear, routes, patches, jnp.asarray(reduction()))


def solution(mesh):
    placed = (
        P(None, ("los", "sky")),
        P("los", None, None, "sky"),
        P("los", None, None, "sky"),
        P(None, None, ("los", "sky"), None),
        P(None, None, ("los", "sky")),
    )
    return jax.shard_map(
        functools.partial(body, mesh.shape["los"], mesh.shape["sky"]),
        mesh=mesh, in_specs=placed, out_specs=P(None, ("los", "sky")), check_vma=False,
    )
```

```python
import functools
import math

import jax
import jax.numpy as jnp
import numpy as np
from jax import lax
from jax.experimental import pallas as pl
from jax.experimental.pallas import tpu as pltpu
from jax.sharding import PartitionSpec as P

MESH = pl.DeviceIdType.MESH
NX, NY, COMPS = 4, 8, 5
CELLS = NX * NY
BASIS = 9
SENT = BASIS * 5
HELD = 48


def reduction():
    i, j = np.arange(NX), np.arange(NY)
    along_x = np.stack([np.ones(NX), np.cos(2 * math.pi * i / NX), np.sin(2 * math.pi * i / NX)])
    along_y = np.stack([np.ones(NY), np.cos(2 * math.pi * j / NY), np.sin(2 * math.pi * j / NY)])
    cells = np.einsum("ai,bj->abij", along_x, along_y).reshape(BASIS, CELLS) / CELLS
    cells[np.abs(cells) < 1e-12] = 0.0
    whole = np.zeros((HELD, COMPS * CELLS), np.float32)
    for ab in range(BASIS):
        for k in range(COMPS):
            whole[ab * COMPS + k, k * CELLS:(k + 1) * CELLS] = cells[ab]
    return whole


def pieces(values, count):
    parts = []
    for _ in range(count):
        part = values.astype(jnp.bfloat16).astype(jnp.float32)
        parts.append(part)
        values = values - part
    return jnp.concatenate(parts, axis=0).astype(jnp.bfloat16)


def cos_turns(turns):
    folded = turns - jnp.floor(turns + 0.5)
    z = (0.25 - jnp.abs(folded)) * (2.0 * math.pi)
    q = z * z
    series = jnp.full_like(q, -1.0 / 39916800.0)
    for term in (1.0 / 362880.0, -1.0 / 5040.0, 1.0 / 120.0, -1.0 / 6.0, 1.0):
        series = series * q + term
    return series * z


def advance(pos, vel, part):
    x, y = pos[0:1] * (1.0 / NX), pos[1:2] * (1.0 / NY)
    wave = cos_turns(jnp.concatenate([x, x - 0.25, y, y - 0.25], axis=0))
    cx, sx, cy, sy = [wave[k:k + 1] for k in range(4)]
    lines = [part[3 * a] + cy * part[3 * a + 1] + sy * part[3 * a + 2] for a in range(3)]
    vals = lines[0] + cx * lines[1] + sx * lines[2]
    p11, p12, p22 = vals[2:3], vals[3:4], vals[4:5]
    top, low = pos[2:4], pos[4:6]
    turn = jnp.concatenate([vals[0:2], p11 * top + p12 * low, p12 * top + p22 * low], axis=0)
    vel = vel - turn
    return pos + 0.5 * vel, vel


def kernel(
    n_los, tiles, hops, halves,
    state_hbm, defl_hbm, shear_hbm, routes_hbm, patches_hbm, reduce_hbm, out_ref,
    state_ref, defl_ref, shear_ref, routes_ref, patches_ref, reduce_ref,
    gathered, tables, looked, outgoing, landed,
    load_sem, send_sem, recv_sem, pass_sem, move_sem, land_sem,
):
    los, sky = lax.axis_index("los"), lax.axis_index("sky")
    rays, cells = state_ref.shape[1], defl_ref.shape[3]
    part_rays = rays // halves
    pair = sky + 1 - 2 * lax.rem(sky, 2)
    peers = [lax.rem(sky + 2 * step, tiles) for step in range(1, tiles // 2)]
    mates = [pair] + [lax.rem(pair + 2 * step, tiles) for step in range(1, tiles // 2)]
    after, before = lax.rem(los + 1, n_los), lax.rem(los + n_los - 1, n_los)

    barrier = pltpu.get_barrier_semaphore()
    friends = [(los, peer) for peer in peers] + [(los, pair), (after, sky), (before, sky)]
    for friend in friends:
        pl.semaphore_signal(barrier, inc=1, device_id=friend, device_id_type=MESH)

    pairs = [
        (reduce_hbm, reduce_ref), (defl_hbm, defl_ref), (shear_hbm, shear_ref),
        (patches_hbm, patches_ref), (routes_hbm, routes_ref), (state_hbm, state_ref),
    ]
    loads = [pltpu.make_async_copy(src, dst, load_sem.at[k]) for k, (src, dst) in enumerate(pairs)]
    for load in loads:
        load.start()
    for load in loads[:3]:
        load.wait()

    def sending(plane, tile, to, sent):
        return pltpu.make_async_remote_copy(
            src_ref=gathered.at[plane, tile], dst_ref=gathered.at[plane, tile],
            send_sem=sent, recv_sem=recv_sem.at[plane, tile],
            device_id=(los, to), device_id_type=MESH,
        )

    started = []
    cut = defl_ref.shape[2]
    lower = pieces(reduce_ref[...], 3)
    for plane in range(2):
        found = jnp.dot(lower[:, :cut], defl_ref[0, plane], preferred_element_type=jnp.float32)
        found += jnp.dot(lower[:, cut:], shear_ref[0, plane], preferred_element_type=jnp.float32)
        found = found[:HELD] + (found[HELD:2 * HELD] + found[2 * HELD:])
        gathered[plane, sky] = found[:SENT]
        if plane == 0:
            pl.semaphore_wait(barrier, len(friends))
        for step, to in enumerate([pair] + peers):
            copy = sending(plane, sky, to, send_sem.at[plane, step])
            copy.start()
            started.append(copy)
    for load in loads[3:]:
        load.wait()

    def build(plane, tile):
        held = jnp.concatenate([gathered[plane, tile], jnp.zeros((HELD - SENT, cells), jnp.float32)], axis=0)
        tables[plane, tile] = pieces(held, 2)

    def from_peers(plane):
        for step, peer in enumerate(peers):
            sending(plane, peer, pair, pass_sem.at[plane, step]).wait_recv()
            copy = sending(plane, peer, pair, pass_sem.at[plane, step])
            copy.start()
            started.append(copy)
        build(plane, sky)
        for peer in peers:
            build(plane, peer)

    def from_pair(plane):
        for mate in mates:
            sending(plane, mate, pair, pass_sem.at[plane, 0]).wait_recv()
            build(plane, mate)

    group = min(tiles, 8)

    def lookup(hop, plane):
        patch = patches_ref[hop, plane:plane + 1, :]
        route = jnp.broadcast_to(routes_ref[2 * hop + plane], (8, rays))
        place = lax.broadcasted_iota(jnp.int32, (cells, rays), 0)
        onehot = jnp.where(place == patch, 1.0, 0.0).astype(jnp.bfloat16)
        chosen = None
        for first in range(0, tiles, group):
            rows = tables[plane, first:first + group].reshape(group * 2 * HELD, cells)
            raw = jnp.dot(rows, onehot, preferred_element_type=jnp.float32)
            raw = raw.reshape(group, 2, HELD // 8, 8, rays)
            for tile in range(group):
                both = raw[tile, 0] + raw[tile, 1]
                named = jnp.broadcast_to(route[None], both.shape) == first + tile
                chosen = both if chosen is None else jnp.where(named, both, chosen)
        looked[hop, plane] = chosen.reshape(HELD, rays)

    def moved(hop, half):
        return pltpu.make_async_remote_copy(
            src_ref=outgoing.at[hop, half], dst_ref=landed.at[hop, half],
            send_sem=move_sem.at[hop, half], recv_sem=land_sem.at[hop, half],
            device_id=(after, sky), device_id_type=MESH,
        )

    def step_plane(hop, plane, half, pos, vel):
        lanes = slice(half * part_rays, (half + 1) * part_rays)
        part = [looked[hop, plane, ab * COMPS:ab * COMPS + 8, lanes] for ab in range(BASIS)]
        return advance(pos, vel, part)

    def parted(state):
        return (
            jnp.concatenate([state[0:2], state[4:8]], axis=0),
            jnp.concatenate([state[2:4], state[8:12]], axis=0),
        )

    def send_on(hop, half, pos, vel):
        outgoing[hop, half, 0:2] = pos[0:2]
        outgoing[hop, half, 2:4] = vel[0:2]
        outgoing[hop, half, 4:8] = pos[2:6]
        outgoing[hop, half, 8:12] = vel[2:6]
        move = moved(hop, half)
        move.start()
        started.append(move)

    from_peers(0)
    from_pair(0)
    lookup(0, 0)
    middle = []
    for half in range(halves):
        pos, vel = parted(state_ref[:, half * part_rays:(half + 1) * part_rays])
        middle.append(step_plane(0, 0, half, pos, vel))
    if hops > 1:
        lookup(1, 0)
    from_peers(1)
    if hops > 2:
        lookup(2, 0)
    from_pair(1)
    lookup(0, 1)
    for half in range(halves):
        send_on(0, half, *step_plane(0, 1, half, *middle[half]))
    for hop in range(1, hops):
        lookup(hop, 1)
        if hop + 2 < hops:
            lookup(hop + 2, 0)
        for half in range(halves):
            moved(hop - 1, half).wait_recv()
            pos, vel = parted(landed[hop - 1, half])
            for plane in range(2):
                pos, vel = step_plane(hop, plane, half, pos, vel)
            send_on(hop, half, pos, vel)
    for half in range(halves):
        moved(hops - 1, half).wait_recv()
        out_ref[:, half * part_rays:(half + 1) * part_rays] = landed[hops - 1, half]
    for copy in started:
        copy.wait_send()


def body(n_los, tiles, state, deflection, shear, routes, patches):
    hops, rays, cells = routes.shape[0], state.shape[1], deflection.shape[3]
    halves = 2
    routes = routes.reshape(hops * 2, 1, rays)
    inputs = (state, deflection, shear, routes, patches, jnp.asarray(reduction()))
    return pl.pallas_call(
        functools.partial(kernel, n_los, tiles, hops, halves),
        out_shape=jax.ShapeDtypeStruct(state.shape, jnp.float32),
        in_specs=[pl.BlockSpec(memory_space=pltpu.HBM)] * 6,
        out_specs=pl.BlockSpec(memory_space=pltpu.VMEM),
        scratch_shapes=[pltpu.VMEM(array.shape, array.dtype) for array in inputs] + [
            pltpu.VMEM((2, tiles, SENT, cells), jnp.float32),
            pltpu.VMEM((2, tiles, 2 * HELD, cells), jnp.bfloat16),
            pltpu.VMEM((hops, 2, HELD, rays), jnp.float32),
            pltpu.VMEM((hops, halves, state.shape[0], rays // halves), jnp.float32),
            pltpu.VMEM((hops, halves, state.shape[0], rays // halves), jnp.float32),
            pltpu.SemaphoreType.DMA((len(inputs),)),
            pltpu.SemaphoreType.DMA((2, tiles // 2)),
            pltpu.SemaphoreType.DMA((2, tiles)),
            pltpu.SemaphoreType.DMA((2, tiles // 2)),
            pltpu.SemaphoreType.DMA((hops, halves)),
            pltpu.SemaphoreType.DMA((hops, halves)),
        ],
        compiler_params=pltpu.CompilerParams(
            collective_id=0, has_side_effects=True, vmem_limit_bytes=64 * 2**20
        ),
    )(*inputs)


def solution(mesh):
    placed = (
        P(None, ("los", "sky")),
        P("los", None, None, "sky"),
        P("los", None, None, "sky"),
        P(None, None, ("los", "sky"), None),
        P(None, None, ("los", "sky")),
    )
    return jax.shard_map(
        functools.partial(body, mesh.shape["los"], mesh.shape["sky"]),
        mesh=mesh, in_specs=placed, out_specs=P(None, ("los", "sky")), check_vma=False,
    )
```

```python
import functools
import math

import jax
import jax.numpy as jnp
import numpy as np
from jax import lax
from jax.experimental import pallas as pl
from jax.experimental.pallas import tpu as pltpu
from jax.sharding import PartitionSpec as P

MESH = pl.DeviceIdType.MESH
NX, NY, COMPS = 4, 8, 5
CELLS = NX * NY
BASIS = 9
SENT = BASIS * 5
HELD = 48


def reduction():
    i, j = np.arange(NX), np.arange(NY)
    along_x = np.stack([np.ones(NX), np.cos(2 * math.pi * i / NX), np.sin(2 * math.pi * i / NX)])
    along_y = np.stack([np.ones(NY), np.cos(2 * math.pi * j / NY), np.sin(2 * math.pi * j / NY)])
    cells = np.einsum("ai,bj->abij", along_x, along_y).reshape(BASIS, CELLS) / CELLS
    cells[np.abs(cells) < 1e-12] = 0.0
    whole = np.zeros((HELD, COMPS * CELLS), np.float32)
    for ab in range(BASIS):
        for k in range(COMPS):
            whole[ab * COMPS + k, k * CELLS:(k + 1) * CELLS] = cells[ab]
    return whole


def pieces(values, count):
    parts = []
    for _ in range(count):
        part = values.astype(jnp.bfloat16).astype(jnp.float32)
        parts.append(part)
        values = values - part
    return [part.astype(jnp.bfloat16) for part in parts]


def cos_turns(turns):
    folded = turns - jnp.floor(turns + 0.5)
    z = (0.25 - jnp.abs(folded)) * (2.0 * math.pi)
    q = z * z
    series = jnp.full_like(q, -1.0 / 39916800.0)
    for term in (1.0 / 362880.0, -1.0 / 5040.0, 1.0 / 120.0, -1.0 / 6.0, 1.0):
        series = series * q + term
    return series * z


def advance(pos, vel, part):
    x, y = pos[0:1] * (1.0 / NX), pos[1:2] * (1.0 / NY)
    wave = cos_turns(jnp.concatenate([x, x - 0.25, y, y - 0.25], axis=0))
    cx, sx, cy, sy = [wave[k:k + 1] for k in range(4)]
    lines = [part[3 * a] + cy * part[3 * a + 1] + sy * part[3 * a + 2] for a in range(3)]
    vals = lines[0] + cx * lines[1] + sx * lines[2]
    p11, p12, p22 = vals[2:3], vals[3:4], vals[4:5]
    top, low = pos[2:4], pos[4:6]
    turn = jnp.concatenate([vals[0:2], p11 * top + p12 * low, p12 * top + p22 * low], axis=0)
    vel = vel - turn
    return pos + 0.5 * vel, vel


def kernel(
    n_los, tiles, hops, halves,
    state_hbm, defl_hbm, shear_hbm, routes_hbm, patches_hbm, reduce_hbm, out_hbm,
    state_ref, defl_ref, shear_ref, routes_ref, patches_ref, reduce_ref,
    gathered, tables, looked, outgoing, landed,
    load_sem, send_sem, recv_sem, pass_sem, move_sem, land_sem, store_sem,
):
    los, sky = lax.axis_index("los"), lax.axis_index("sky")
    rays, cells = state_ref.shape[1], defl_ref.shape[3]
    part_rays = rays // halves
    pair = sky + 1 - 2 * lax.rem(sky, 2)
    peers = [lax.rem(sky + 2 * step, tiles) for step in range(1, tiles // 2)]
    mates = [pair] + [lax.rem(pair + 2 * step, tiles) for step in range(1, tiles // 2)]
    after, before = lax.rem(los + 1, n_los), lax.rem(los + n_los - 1, n_los)

    barrier = pltpu.get_barrier_semaphore()
    friends = [(los, peer) for peer in peers] + [(los, pair), (after, sky), (before, sky)]
    for friend in friends:
        pl.semaphore_signal(barrier, inc=1, device_id=friend, device_id_type=MESH)

    pairs = [
        (reduce_hbm, reduce_ref), (defl_hbm, defl_ref), (shear_hbm, shear_ref),
        (patches_hbm, patches_ref), (routes_hbm, routes_ref), (state_hbm, state_ref),
    ]
    loads = [pltpu.make_async_copy(src, dst, load_sem.at[k]) for k, (src, dst) in enumerate(pairs)]
    for load in loads:
        load.start()
    for load in loads[:3]:
        load.wait()

    def sending(plane, tile, to, sent):
        return pltpu.make_async_remote_copy(
            src_ref=gathered.at[plane, tile], dst_ref=gathered.at[plane, tile],
            send_sem=sent, recv_sem=recv_sem.at[plane, tile],
            device_id=(los, to), device_id_type=MESH,
        )

    started = []
    cut = defl_ref.shape[2]
    lower = jnp.concatenate(pieces(reduce_ref[...], 3), axis=0)
    for plane in range(2):
        found = jnp.dot(lower[:, :cut], defl_ref[0, plane], preferred_element_type=jnp.float32)
        found += jnp.dot(lower[:, cut:], shear_ref[0, plane], preferred_element_type=jnp.float32)
        found = found[:HELD] + (found[HELD:2 * HELD] + found[2 * HELD:])
        gathered[plane, sky] = found[:SENT]
        if plane == 0:
            pl.semaphore_wait(barrier, len(friends))
        for step, to in enumerate([pair] + peers):
            if plane == 1:
                started[step].wait_send()
            copy = sending(plane, sky, to, send_sem.at[plane, step])
            copy.start()
            started.append(copy)
    started = started[tiles // 2:]
    for load in loads[3:]:
        load.wait()

    half_tiles = tiles // 2
    own = lax.rem(sky, 2)

    def build(plane, tile, other):
        held = jnp.concatenate([gathered[plane, tile], jnp.zeros((HELD - SENT, cells), jnp.float32)], axis=0)
        high, low = pieces(held, 2)
        tables[plane, other, tile // 2, :, :cells] = high
        tables[plane, other, tile // 2, :, cells:] = low

    def from_peers(plane):
        for step, peer in enumerate(peers):
            sending(plane, peer, pair, pass_sem.at[plane, step]).wait_recv()
            copy = sending(plane, peer, pair, pass_sem.at[plane, step])
            copy.start()
            started.append(copy)
        build(plane, sky, 0)
        for peer in peers:
            build(plane, peer, 0)

    def from_pair(plane):
        for mate in mates:
            sending(plane, mate, pair, pass_sem.at[plane, 0]).wait_recv()
            build(plane, mate, 1)

    group = min(half_tiles, 8)

    def lookup(hop, plane, others=(0, 1)):
        patch = patches_ref[hop, plane:plane + 1, :]
        route = jnp.broadcast_to(routes_ref[2 * hop + plane], (8, rays))
        place = lax.broadcasted_iota(jnp.int32, (cells, rays), 0)
        onehot = jnp.where(place == patch, 1.0, 0.0).astype(jnp.bfloat16)
        onehot = jnp.concatenate([onehot, onehot], axis=0)
        chosen = None if others[0] == 0 else looked[hop, plane].reshape(HELD // 8, 8, rays)
        for other in others:
            core = own if other == 0 else 1 - own
            for first in range(0, half_tiles, group):
                rows = tables[plane, other, first:first + group].reshape(group * HELD, 2 * cells)
                raw = jnp.dot(rows, onehot, preferred_element_type=jnp.float32)
                raw = raw.reshape(group, HELD // 8, 8, rays)
                for k in range(group):
                    named = jnp.broadcast_to(route[None], raw[k].shape) == 2 * (first + k) + core
                    chosen = raw[k] if chosen is None else jnp.where(named, raw[k], chosen)
        looked[hop, plane] = chosen.reshape(HELD, rays)

    def moved(hop, half):
        return pltpu.make_async_remote_copy(
            src_ref=outgoing.at[hop, half], dst_ref=landed.at[hop, half],
            send_sem=move_sem.at[hop, half], recv_sem=land_sem.at[hop, half],
            device_id=(after, sky), device_id_type=MESH,
        )

    def step_plane(hop, plane, half, pos, vel):
        lanes = slice(half * part_rays, (half + 1) * part_rays)
        part = [looked[hop, plane, ab * COMPS:ab * COMPS + 8, lanes] for ab in range(BASIS)]
        return advance(pos, vel, part)

    def parted(state):
        return (
            jnp.concatenate([state[0:2], state[4:8]], axis=0),
            jnp.concatenate([state[2:4], state[8:12]], axis=0),
        )

    def send_on(hop, half, pos, vel):
        outgoing[hop, half, 0:2] = pos[0:2]
        outgoing[hop, half, 2:4] = vel[0:2]
        outgoing[hop, half, 4:8] = pos[2:6]
        outgoing[hop, half, 8:12] = vel[2:6]
        move = moved(hop, half)
        move.start()
        started.append(move)

    from_peers(0)
    lookup(0, 0, (0,))
    from_pair(0)
    lookup(0, 0, (1,))
    middle = []
    for half in range(halves):
        pos, vel = parted(state_ref[:, half * part_rays:(half + 1) * part_rays])
        middle.append(step_plane(0, 0, half, pos, vel))
    if hops > 1:
        lookup(1, 0)
    from_peers(1)
    lookup(0, 1, (0,))
    from_pair(1)
    lookup(0, 1, (1,))
    for half in range(halves):
        send_on(0, half, *step_plane(0, 1, half, *middle[half]))
    for hop in range(1, hops):
        lookup(hop, 1)
        if hop > 1:
            lookup(hop, 0)
        for half in range(halves):
            moved(hop - 1, half).wait_recv()
            pos, vel = parted(landed[hop - 1, half])
            for plane in range(2):
                pos, vel = step_plane(hop, plane, half, pos, vel)
            send_on(hop, half, pos, vel)
    stores = []
    for half in range(halves):
        moved(hops - 1, half).wait_recv()
        lanes = pl.ds(half * part_rays, part_rays)
        store = pltpu.make_async_copy(landed.at[hops - 1, half], out_hbm.at[:, lanes], store_sem.at[half])
        store.start()
        stores.append(store)
    for copy in started:
        copy.wait_send()
    for store in stores:
        store.wait()


def body(n_los, tiles, state, deflection, shear, routes, patches):
    hops, rays, cells = routes.shape[0], state.shape[1], deflection.shape[3]
    halves = 2
    routes = routes.reshape(hops * 2, 1, rays)
    inputs = (state, deflection, shear, routes, patches, jnp.asarray(reduction()))
    return pl.pallas_call(
        functools.partial(kernel, n_los, tiles, hops, halves),
        out_shape=jax.ShapeDtypeStruct(state.shape, jnp.float32),
        in_specs=[pl.BlockSpec(memory_space=pltpu.HBM)] * 6,
        out_specs=pl.BlockSpec(memory_space=pltpu.HBM),
        scratch_shapes=[pltpu.VMEM(array.shape, array.dtype) for array in inputs] + [
            pltpu.VMEM((2, tiles, SENT, cells), jnp.float32),
            pltpu.VMEM((2, 2, tiles // 2, HELD, 2 * cells), jnp.bfloat16),
            pltpu.VMEM((hops, 2, HELD, rays), jnp.float32),
            pltpu.VMEM((hops, halves, state.shape[0], rays // halves), jnp.float32),
            pltpu.VMEM((hops, halves, state.shape[0], rays // halves), jnp.float32),
            pltpu.SemaphoreType.DMA((len(inputs),)),
            pltpu.SemaphoreType.DMA((2, tiles // 2)),
            pltpu.SemaphoreType.DMA((2, tiles)),
            pltpu.SemaphoreType.DMA((2, tiles // 2)),
            pltpu.SemaphoreType.DMA((hops, halves)),
            pltpu.SemaphoreType.DMA((hops, halves)),
            pltpu.SemaphoreType.DMA((halves,)),
        ],
        compiler_params=pltpu.CompilerParams(
            collective_id=0, has_side_effects=True, vmem_limit_bytes=64 * 2**20
        ),
    )(*inputs)


def solution(mesh):
    placed = (
        P(None, ("los", "sky")),
        P("los", None, None, "sky"),
        P("los", None, None, "sky"),
        P(None, None, ("los", "sky"), None),
        P(None, None, ("los", "sky")),
    )
    return jax.shard_map(
        functools.partial(body, mesh.shape["los"], mesh.shape["sky"]),
        mesh=mesh, in_specs=placed, out_specs=P(None, ("los", "sky")), check_vma=False,
    )
```

```python
import functools
import math

import jax
import jax.numpy as jnp
import numpy as np
from jax import lax
from jax.experimental import pallas as pl
from jax.experimental.pallas import tpu as pltpu
from jax.sharding import PartitionSpec as P

MESH = pl.DeviceIdType.MESH
NX, NY, COMPS = 4, 8, 5
CELLS = NX * NY
BASIS = 9
SENT = BASIS * 5
HELD = 48


def reduction():
    i, j = np.arange(NX), np.arange(NY)
    along_x = np.stack([np.ones(NX), np.cos(2 * math.pi * i / NX), np.sin(2 * math.pi * i / NX)])
    along_y = np.stack([np.ones(NY), np.cos(2 * math.pi * j / NY), np.sin(2 * math.pi * j / NY)])
    cells = np.einsum("ai,bj->abij", along_x, along_y).reshape(BASIS, CELLS) / CELLS
    cells[np.abs(cells) < 1e-12] = 0.0
    whole = np.zeros((HELD, COMPS * CELLS), np.float32)
    for ab in range(BASIS):
        for k in range(COMPS):
            whole[ab * COMPS + k, k * CELLS:(k + 1) * CELLS] = cells[ab]
    return whole


def pieces(values, count):
    parts = []
    for _ in range(count):
        part = values.astype(jnp.bfloat16).astype(jnp.float32)
        parts.append(part)
        values = values - part
    return [part.astype(jnp.bfloat16) for part in parts]


def cos_turns(turns):
    folded = turns - jnp.floor(turns + 0.5)
    z = (0.25 - jnp.abs(folded)) * (2.0 * math.pi)
    q = z * z
    series = jnp.full_like(q, -1.0 / 39916800.0)
    for term in (1.0 / 362880.0, -1.0 / 5040.0, 1.0 / 120.0, -1.0 / 6.0, 1.0):
        series = series * q + term
    return series * z


def advance(pos, vel, part):
    x, y = pos[0:1] * (1.0 / NX), pos[1:2] * (1.0 / NY)
    wave = cos_turns(jnp.concatenate([x, x - 0.25, y, y - 0.25], axis=0))
    cx, sx, cy, sy = [wave[k:k + 1] for k in range(4)]
    lines = [part[3 * a] + cy * part[3 * a + 1] + sy * part[3 * a + 2] for a in range(3)]
    vals = lines[0] + cx * lines[1] + sx * lines[2]
    p11, p12, p22 = vals[2:3], vals[3:4], vals[4:5]
    top, low = pos[2:4], pos[4:6]
    turn = jnp.concatenate([vals[0:2], p11 * top + p12 * low, p12 * top + p22 * low], axis=0)
    vel = vel - turn
    return pos + 0.5 * vel, vel


def kernel(
    n_los, tiles, hops, halves,
    state_hbm, defl_hbm, shear_hbm, routes_hbm, patches_hbm, reduce_hbm, out_hbm,
    state_ref, defl_ref, shear_ref, routes_ref, patches_ref, reduce_ref,
    gathered, tables, looked, lent, outgoing, landed,
    load_sem, send_sem, recv_sem, pass_sem, move_sem, land_sem, lend_sem, lent_sem, store_sem,
):
    los, sky = lax.axis_index("los"), lax.axis_index("sky")
    rays, cells = state_ref.shape[1], defl_ref.shape[3]
    part_rays = rays // halves
    pair = sky + 1 - 2 * lax.rem(sky, 2)
    peers = [lax.rem(sky + 2 * step, tiles) for step in range(1, tiles // 2)]
    mates = [pair] + [lax.rem(pair + 2 * step, tiles) for step in range(1, tiles // 2)]
    after, before = lax.rem(los + 1, n_los), lax.rem(los + n_los - 1, n_los)

    barrier = pltpu.get_barrier_semaphore()
    home = lax.rem(los + 2, n_los)
    friends = [(los, peer) for peer in peers] + [(los, pair), (after, sky), (before, sky), (home, sky)]
    if n_los != 4:
        friends.append((lax.rem(los + n_los - 2, n_los), sky))
    for friend in friends:
        pl.semaphore_signal(barrier, inc=1, device_id=friend, device_id_type=MESH)

    pairs = [
        (reduce_hbm, reduce_ref), (defl_hbm, defl_ref), (shear_hbm, shear_ref),
        (patches_hbm, patches_ref), (routes_hbm, routes_ref), (state_hbm, state_ref),
    ]
    loads = [pltpu.make_async_copy(src, dst, load_sem.at[k]) for k, (src, dst) in enumerate(pairs)]
    for load in loads:
        load.start()
    for load in loads[:3]:
        load.wait()

    def sending(plane, tile, to, sent):
        return pltpu.make_async_remote_copy(
            src_ref=gathered.at[plane, tile], dst_ref=gathered.at[plane, tile],
            send_sem=sent, recv_sem=recv_sem.at[plane, tile],
            device_id=(los, to), device_id_type=MESH,
        )

    started = []
    cut = defl_ref.shape[2]
    lower = jnp.concatenate(pieces(reduce_ref[...], 3), axis=0)
    for plane in range(2):
        found = jnp.dot(lower[:, :cut], defl_ref[0, plane], preferred_element_type=jnp.float32)
        found += jnp.dot(lower[:, cut:], shear_ref[0, plane], preferred_element_type=jnp.float32)
        found = found[:HELD] + (found[HELD:2 * HELD] + found[2 * HELD:])
        gathered[plane, sky] = found[:SENT]
        if plane == 0:
            pl.semaphore_wait(barrier, len(friends))
        for step, to in enumerate([pair] + peers):
            if plane == 1:
                started[step].wait_send()
            copy = sending(plane, sky, to, send_sem.at[plane, step])
            copy.start()
            started.append(copy)
    started = started[tiles // 2:]
    for load in loads[3:]:
        load.wait()

    half_tiles = tiles // 2
    own = lax.rem(sky, 2)

    def build(plane, tile, other):
        held = jnp.concatenate([gathered[plane, tile], jnp.zeros((HELD - SENT, cells), jnp.float32)], axis=0)
        high, low = pieces(held, 2)
        tables[plane, other, tile // 2, :, :cells] = high
        tables[plane, other, tile // 2, :, cells:] = low

    def from_peers(plane):
        for step, peer in enumerate(peers):
            sending(plane, peer, pair, pass_sem.at[plane, step]).wait_recv()
            copy = sending(plane, peer, pair, pass_sem.at[plane, step])
            copy.start()
            started.append(copy)
        build(plane, sky, 0)
        for peer in peers:
            build(plane, peer, 0)

    def from_pair(plane):
        for mate in mates:
            sending(plane, mate, pair, pass_sem.at[plane, 0]).wait_recv()
            build(plane, mate, 1)

    group = min(half_tiles, 8)

    def lookup(hop, plane, others=(0, 1)):
        patch = patches_ref[hop, plane:plane + 1, :]
        route = jnp.broadcast_to(routes_ref[2 * hop + plane], (8, rays))
        place = lax.broadcasted_iota(jnp.int32, (cells, rays), 0)
        onehot = jnp.where(place == patch, 1.0, 0.0).astype(jnp.bfloat16)
        onehot = jnp.concatenate([onehot, onehot], axis=0)
        chosen = None if others[0] == 0 else looked[hop, plane].reshape(HELD // 8, 8, rays)
        for other in others:
            core = own if other == 0 else 1 - own
            for first in range(0, half_tiles, group):
                rows = tables[plane, other, first:first + group].reshape(group * HELD, 2 * cells)
                raw = jnp.dot(rows, onehot, preferred_element_type=jnp.float32)
                raw = raw.reshape(group, HELD // 8, 8, rays)
                for k in range(group):
                    named = jnp.broadcast_to(route[None], raw[k].shape) == 2 * (first + k) + core
                    chosen = raw[k] if chosen is None else jnp.where(named, raw[k], chosen)
        looked[hop, plane] = chosen.reshape(HELD, rays)

    def moved(hop, half):
        return pltpu.make_async_remote_copy(
            src_ref=outgoing.at[hop, half], dst_ref=landed.at[hop, half],
            send_sem=move_sem.at[hop, half], recv_sem=land_sem.at[hop, half],
            device_id=(after if hop < hops - 2 else home, sky), device_id_type=MESH,
        )

    def lending(plane):
        return pltpu.make_async_remote_copy(
            src_ref=looked.at[hops - 1, plane], dst_ref=lent.at[plane],
            send_sem=lend_sem.at[plane], recv_sem=lent_sem.at[plane],
            device_id=(after, sky), device_id_type=MESH,
        )

    def lend(plane):
        lookup(hops - 1, plane)
        copy = lending(plane)
        copy.start()
        started.append(copy)

    def step_plane(hop, plane, half, pos, vel):
        lanes = slice(half * part_rays, (half + 1) * part_rays)
        table = looked.at[hop, plane] if hop < hops - 1 else lent.at[plane]
        part = [table[ab * COMPS:ab * COMPS + 8, lanes] for ab in range(BASIS)]
        return advance(pos, vel, part)

    def parted(state):
        return (
            jnp.concatenate([state[0:2], state[4:8]], axis=0),
            jnp.concatenate([state[2:4], state[8:12]], axis=0),
        )

    def send_on(hop, half, pos, vel):
        outgoing[hop, half, 0:2] = pos[0:2]
        outgoing[hop, half, 2:4] = vel[0:2]
        outgoing[hop, half, 4:8] = pos[2:6]
        outgoing[hop, half, 8:12] = vel[2:6]
        if hop == hops - 1:
            lanes = pl.ds(half * part_rays, part_rays)
            store = pltpu.make_async_copy(outgoing.at[hop, half], out_hbm.at[:, lanes], store_sem.at[half])
            store.start()
            stores.append(store)
            return
        move = moved(hop, half)
        move.start()
        started.append(move)

    from_peers(0)
    lookup(0, 0, (0,))
    from_pair(0)
    lookup(0, 0, (1,))
    middle, stores = [], []
    for half in range(halves):
        pos, vel = parted(state_ref[:, half * part_rays:(half + 1) * part_rays])
        middle.append(step_plane(0, 0, half, pos, vel))
    lend(0)
    from_peers(1)
    lookup(0, 1, (0,))
    from_pair(1)
    lookup(0, 1, (1,))
    for half in range(halves):
        send_on(0, half, *step_plane(0, 1, half, *middle[half]))
    lend(1)
    for hop in range(1, hops):
        for plane in range(2):
            if hop < hops - 1:
                lookup(hop, plane)
            else:
                lending(plane).wait_recv()
        for half in range(halves):
            moved(hop - 1, half).wait_recv()
            pos, vel = parted(landed[hop - 1, half])
            for plane in range(2):
                pos, vel = step_plane(hop, plane, half, pos, vel)
            send_on(hop, half, pos, vel)
    for copy in started:
        copy.wait_send()
    for store in stores:
        store.wait()


def body(n_los, tiles, state, deflection, shear, routes, patches):
    hops, rays, cells = routes.shape[0], state.shape[1], deflection.shape[3]
    halves = 2
    routes = routes.reshape(hops * 2, 1, rays)
    inputs = (state, deflection, shear, routes, patches, jnp.asarray(reduction()))
    return pl.pallas_call(
        functools.partial(kernel, n_los, tiles, hops, halves),
        out_shape=jax.ShapeDtypeStruct(state.shape, jnp.float32),
        in_specs=[pl.BlockSpec(memory_space=pltpu.HBM)] * 6,
        out_specs=pl.BlockSpec(memory_space=pltpu.HBM),
        scratch_shapes=[pltpu.VMEM(array.shape, array.dtype) for array in inputs] + [
            pltpu.VMEM((2, tiles, SENT, cells), jnp.float32),
            pltpu.VMEM((2, 2, tiles // 2, HELD, 2 * cells), jnp.bfloat16),
            pltpu.VMEM((hops, 2, HELD, rays), jnp.float32),
            pltpu.VMEM((2, HELD, rays), jnp.float32),
            pltpu.VMEM((hops, halves, state.shape[0], rays // halves), jnp.float32),
            pltpu.VMEM((hops - 1, halves, state.shape[0], rays // halves), jnp.float32),
            pltpu.SemaphoreType.DMA((len(inputs),)),
            pltpu.SemaphoreType.DMA((2, tiles // 2)),
            pltpu.SemaphoreType.DMA((2, tiles)),
            pltpu.SemaphoreType.DMA((2, tiles // 2)),
            pltpu.SemaphoreType.DMA((hops - 1, halves)),
            pltpu.SemaphoreType.DMA((hops - 1, halves)),
            pltpu.SemaphoreType.DMA((2,)),
            pltpu.SemaphoreType.DMA((2,)),
            pltpu.SemaphoreType.DMA((halves,)),
        ],
        compiler_params=pltpu.CompilerParams(
            collective_id=0, has_side_effects=True, vmem_limit_bytes=64 * 2**20
        ),
    )(*inputs)


def solution(mesh):
    placed = (
        P(None, ("los", "sky")),
        P("los", None, None, "sky"),
        P("los", None, None, "sky"),
        P(None, None, ("los", "sky"), None),
        P(None, None, ("los", "sky")),
    )
    return jax.shard_map(
        functools.partial(body, mesh.shape["los"], mesh.shape["sky"]),
        mesh=mesh, in_specs=placed, out_specs=P(None, ("los", "sky")), check_vma=False,
    )
```

```python
import functools
import math

import jax
import jax.numpy as jnp
import numpy as np
from jax import lax
from jax.experimental import pallas as pl
from jax.experimental.pallas import tpu as pltpu
from jax.sharding import PartitionSpec as P

MESH = pl.DeviceIdType.MESH
NX, NY, COMPS = 4, 8, 5
CELLS = NX * NY
BASIS = 9
SENT = BASIS * 5
HELD = 48


def reduction():
    i, j = np.arange(NX), np.arange(NY)
    along_x = np.stack([np.ones(NX), np.cos(2 * math.pi * i / NX), np.sin(2 * math.pi * i / NX)])
    along_y = np.stack([np.ones(NY), np.cos(2 * math.pi * j / NY), np.sin(2 * math.pi * j / NY)])
    cells = np.einsum("ai,bj->abij", along_x, along_y).reshape(BASIS, CELLS) / CELLS
    cells[np.abs(cells) < 1e-12] = 0.0
    whole = np.zeros((HELD, COMPS * CELLS), np.float32)
    for ab in range(BASIS):
        for k in range(COMPS):
            whole[ab * COMPS + k, k * CELLS:(k + 1) * CELLS] = cells[ab]
    return whole


def pieces(values, count):
    parts = []
    for _ in range(count):
        part = values.astype(jnp.bfloat16).astype(jnp.float32)
        parts.append(part)
        values = values - part
    return [part.astype(jnp.bfloat16) for part in parts]


def cos_turns(turns):
    folded = turns - jnp.floor(turns + 0.5)
    z = (0.25 - jnp.abs(folded)) * (2.0 * math.pi)
    q = z * z
    series = jnp.full_like(q, -1.0 / 39916800.0)
    for term in (1.0 / 362880.0, -1.0 / 5040.0, 1.0 / 120.0, -1.0 / 6.0, 1.0):
        series = series * q + term
    return series * z


def advance(pos, vel, part):
    x, y = pos[0:1] * (1.0 / NX), pos[1:2] * (1.0 / NY)
    wave = cos_turns(jnp.concatenate([x, x - 0.25, y, y - 0.25], axis=0))
    cx, sx, cy, sy = [wave[k:k + 1] for k in range(4)]
    lines = [part[3 * a] + cy * part[3 * a + 1] + sy * part[3 * a + 2] for a in range(3)]
    vals = lines[0] + cx * lines[1] + sx * lines[2]
    p11, p12, p22 = vals[2:3], vals[3:4], vals[4:5]
    top, low = pos[2:4], pos[4:6]
    turn = jnp.concatenate([vals[0:2], p11 * top + p12 * low, p12 * top + p22 * low], axis=0)
    vel = vel - turn
    return pos + 0.5 * vel, vel


def kernel(
    n_los, tiles, hops, halves,
    state_hbm, defl_hbm, shear_hbm, routes_hbm, patches_hbm, reduce_hbm, out_hbm,
    state_ref, defl_ref, shear_ref, routes_ref, patches_ref, reduce_ref,
    gathered, tables, looked, outgoing, landed,
    load_sem, send_sem, recv_sem, pass_sem, move_sem, land_sem, store_sem,
):
    los, sky = lax.axis_index("los"), lax.axis_index("sky")
    rays, cells = state_ref.shape[1], defl_ref.shape[3]
    part_rays = rays // halves
    pair = sky + 1 - 2 * lax.rem(sky, 2)
    peers = [lax.rem(sky + 2 * step, tiles) for step in range(1, tiles // 2)]
    mates = [pair] + [lax.rem(pair + 2 * step, tiles) for step in range(1, tiles // 2)]
    after, before = lax.rem(los + 1, n_los), lax.rem(los + n_los - 1, n_los)

    barrier = pltpu.get_barrier_semaphore()
    friends = [(los, peer) for peer in peers] + [(los, pair), (after, sky), (before, sky)]
    for friend in friends:
        pl.semaphore_signal(barrier, inc=1, device_id=friend, device_id_type=MESH)

    pairs = [
        (reduce_hbm, reduce_ref), (defl_hbm, defl_ref), (shear_hbm, shear_ref),
        (patches_hbm, patches_ref), (routes_hbm, routes_ref), (state_hbm, state_ref),
    ]
    loads = [pltpu.make_async_copy(src, dst, load_sem.at[k]) for k, (src, dst) in enumerate(pairs)]
    for load in loads:
        load.start()
    for load in loads[:3]:
        load.wait()

    def sending(plane, tile, to, sent):
        return pltpu.make_async_remote_copy(
            src_ref=gathered.at[plane, tile], dst_ref=gathered.at[plane, tile],
            send_sem=sent, recv_sem=recv_sem.at[plane, tile],
            device_id=(los, to), device_id_type=MESH,
        )

    started = []
    cut = defl_ref.shape[2]
    lower = jnp.concatenate(pieces(reduce_ref[...], 3), axis=0)
    for plane in range(2):
        found = jnp.dot(lower[:, :cut], defl_ref[0, plane], preferred_element_type=jnp.float32)
        found += jnp.dot(lower[:, cut:], shear_ref[0, plane], preferred_element_type=jnp.float32)
        found = found[:HELD] + (found[HELD:2 * HELD] + found[2 * HELD:])
        gathered[plane, sky] = found[:SENT]
        if plane == 0:
            pl.semaphore_wait(barrier, len(friends))
        for step, to in enumerate([pair] + peers):
            if plane == 1:
                started[step].wait_send()
            copy = sending(plane, sky, to, send_sem.at[plane, step])
            copy.start()
            started.append(copy)
    started = started[tiles // 2:]
    for load in loads[3:]:
        load.wait()

    half_tiles = tiles // 2
    own = lax.rem(sky, 2)

    def build(plane, tile, other):
        held = jnp.concatenate([gathered[plane, tile], jnp.zeros((HELD - SENT, cells), jnp.float32)], axis=0)
        high, low = pieces(held, 2)
        tables[plane, other, tile // 2, :, :cells] = high
        tables[plane, other, tile // 2, :, cells:] = low

    def from_peers(plane):
        for step, peer in enumerate(peers):
            sending(plane, peer, pair, pass_sem.at[plane, step]).wait_recv()
            sending(plane, peer, pair, pass_sem.at[plane, step]).start()
        build(plane, sky, 0)
        for peer in peers:
            build(plane, peer, 0)

    def from_pair(plane):
        for mate in mates:
            sending(plane, mate, pair, pass_sem.at[plane, 0]).wait_recv()
            build(plane, mate, 1)

    group = min(half_tiles, 8)

    block = min(rays, 512)

    def lookup(hop, plane, others=(0, 1)):
        def lookup_block(index, carry):
            lanes = pl.ds(pl.multiple_of(index * block, block), block)
            both = patches_ref[hop, :, lanes]
            patch = jnp.where(plane == 0, both[0:1], both[1:2])
            route = jnp.broadcast_to(routes_ref[2 * hop + plane, :, lanes], (8, block))
            place = lax.broadcasted_iota(jnp.int32, (cells, block), 0)
            onehot = jnp.where(place == patch, 1.0, 0.0).astype(jnp.bfloat16)
            onehot = jnp.concatenate([onehot, onehot], axis=0)
            chosen = None
            if others[0] != 0:
                chosen = looked[hop, plane, :, lanes].reshape(HELD // 8, 8, block)
            for other in others:
                core = own if other == 0 else 1 - own
                for first in range(0, half_tiles, group):
                    rows = tables[plane, other, first:first + group].reshape(group * HELD, 2 * cells)
                    raw = jnp.dot(rows, onehot, preferred_element_type=jnp.float32)
                    raw = raw.reshape(group, HELD // 8, 8, block)
                    for k in range(group):
                        named = jnp.broadcast_to(route[None], raw[k].shape) == 2 * (first + k) + core
                        chosen = raw[k] if chosen is None else jnp.where(named, raw[k], chosen)
            looked[hop, plane, :, lanes] = chosen.reshape(HELD, block)
            return carry

        lax.fori_loop(0, rays // block, lookup_block, 0)

    def moved(hop, half):
        return pltpu.make_async_remote_copy(
            src_ref=outgoing.at[hop, half], dst_ref=landed.at[hop, half],
            send_sem=move_sem.at[hop, half], recv_sem=land_sem.at[hop, half],
            device_id=(after, sky), device_id_type=MESH,
        )

    def step_plane(hop, plane, half, pos, vel):
        lanes = slice(half * part_rays, (half + 1) * part_rays)
        part = [looked[hop, plane, ab * COMPS:ab * COMPS + 8, lanes] for ab in range(BASIS)]
        return advance(pos, vel, part)

    def parted(state):
        return (
            jnp.concatenate([state[0:2], state[4:8]], axis=0),
            jnp.concatenate([state[2:4], state[8:12]], axis=0),
        )

    def send_on(hop, half, pos, vel):
        outgoing[hop, half, 0:2] = pos[0:2]
        outgoing[hop, half, 2:4] = vel[0:2]
        outgoing[hop, half, 4:8] = pos[2:6]
        outgoing[hop, half, 8:12] = vel[2:6]
        moved(hop, half).start()

    def first_hop(plane, rays_now):
        from_peers(plane)
        lookup(0, plane, (0,))
        from_pair(plane)
        lookup(0, plane, (1,))
        return tuple(step_plane(0, plane, half, *rays_now[half]) for half in range(halves))

    at_start = tuple(
        parted(state_ref[:, half * part_rays:(half + 1) * part_rays]) for half in range(halves)
    )
    after_first = lax.fori_loop(0, 2, first_hop, at_start)
    for half in range(halves):
        send_on(0, half, *after_first[half])

    def later_hop(hop, carry):
        def both_planes(plane, inner):
            lookup(hop, plane)
            return inner

        lax.fori_loop(0, 2, both_planes, 0)
        for half in range(halves):
            moved(hop - 1, half).wait_recv()
            rays_now = parted(landed[hop - 1, half])
            for plane in range(2):
                rays_now = step_plane(hop, plane, half, *rays_now)
            send_on(hop, half, *rays_now)
        return carry

    lax.fori_loop(1, hops, later_hop, 0)
    stores = []
    for half in range(halves):
        moved(hops - 1, half).wait_recv()
        lanes = pl.ds(half * part_rays, part_rays)
        store = pltpu.make_async_copy(landed.at[hops - 1, half], out_hbm.at[:, lanes], store_sem.at[half])
        store.start()
        stores.append(store)
    for copy in started:
        copy.wait_send()
    for plane in range(2):
        for step, peer in enumerate(peers):
            sending(plane, peer, pair, pass_sem.at[plane, step]).wait_send()
    for hop in range(hops):
        for half in range(halves):
            moved(hop, half).wait_send()
    for store in stores:
        store.wait()


def body(n_los, tiles, state, deflection, shear, routes, patches):
    hops, rays, cells = routes.shape[0], state.shape[1], deflection.shape[3]
    halves = 2
    routes = routes.reshape(hops * 2, 1, rays)
    inputs = (state, deflection, shear, routes, patches, jnp.asarray(reduction()))
    return pl.pallas_call(
        functools.partial(kernel, n_los, tiles, hops, halves),
        out_shape=jax.ShapeDtypeStruct(state.shape, jnp.float32),
        in_specs=[pl.BlockSpec(memory_space=pltpu.HBM)] * 6,
        out_specs=pl.BlockSpec(memory_space=pltpu.HBM),
        scratch_shapes=[pltpu.VMEM(array.shape, array.dtype) for array in inputs] + [
            pltpu.VMEM((2, tiles, SENT, cells), jnp.float32),
            pltpu.VMEM((2, 2, tiles // 2, HELD, 2 * cells), jnp.bfloat16),
            pltpu.VMEM((hops, 2, HELD, rays), jnp.float32),
            pltpu.VMEM((hops, halves, state.shape[0], rays // halves), jnp.float32),
            pltpu.VMEM((hops, halves, state.shape[0], rays // halves), jnp.float32),
            pltpu.SemaphoreType.DMA((len(inputs),)),
            pltpu.SemaphoreType.DMA((2, tiles // 2)),
            pltpu.SemaphoreType.DMA((2, tiles)),
            pltpu.SemaphoreType.DMA((2, tiles // 2)),
            pltpu.SemaphoreType.DMA((hops, halves)),
            pltpu.SemaphoreType.DMA((hops, halves)),
            pltpu.SemaphoreType.DMA((halves,)),
        ],
        compiler_params=pltpu.CompilerParams(
            collective_id=0, has_side_effects=True, vmem_limit_bytes=64 * 2**20
        ),
    )(*inputs)


def solution(mesh):
    placed = (
        P(None, ("los", "sky")),
        P("los", None, None, "sky"),
        P("los", None, None, "sky"),
        P(None, None, ("los", "sky"), None),
        P(None, None, ("los", "sky")),
    )
    return jax.shard_map(
        functools.partial(body, mesh.shape["los"], mesh.shape["sky"]),
        mesh=mesh, in_specs=placed, out_specs=P(None, ("los", "sky")), check_vma=False,
    )
```

```python
import functools
import math

import jax
import jax.numpy as jnp
import numpy as np
from jax import lax
from jax.experimental import pallas as pl
from jax.experimental.pallas import tpu as pltpu
from jax.sharding import PartitionSpec as P

MESH = pl.DeviceIdType.MESH
NX, NY, COMPS = 4, 8, 5
CELLS = NX * NY
BASIS = 9
SENT = BASIS * 5
HELD = 48


def reduction():
    i, j = np.arange(NX), np.arange(NY)
    along_x = np.stack([np.ones(NX), np.cos(2 * math.pi * i / NX), np.sin(2 * math.pi * i / NX)])
    along_y = np.stack([np.ones(NY), np.cos(2 * math.pi * j / NY), np.sin(2 * math.pi * j / NY)])
    cells = np.einsum("ai,bj->abij", along_x, along_y).reshape(BASIS, CELLS) / CELLS
    cells[np.abs(cells) < 1e-12] = 0.0
    whole = np.zeros((HELD, COMPS * CELLS), np.float32)
    for ab in range(BASIS):
        for k in range(COMPS):
            whole[ab * COMPS + k, k * CELLS:(k + 1) * CELLS] = cells[ab]
    return whole


def pieces(values, count):
    parts = []
    for _ in range(count):
        part = values.astype(jnp.bfloat16).astype(jnp.float32)
        parts.append(part)
        values = values - part
    return [part.astype(jnp.bfloat16) for part in parts]


def cos_turns(turns):
    folded = turns - jnp.floor(turns + 0.5)
    z = (0.25 - jnp.abs(folded)) * (2.0 * math.pi)
    q = z * z
    series = jnp.full_like(q, -1.0 / 39916800.0)
    for term in (1.0 / 362880.0, -1.0 / 5040.0, 1.0 / 120.0, -1.0 / 6.0, 1.0):
        series = series * q + term
    return series * z


def advance(pos, vel, part):
    x, y = pos[0:1] * (1.0 / NX), pos[1:2] * (1.0 / NY)
    wave = cos_turns(jnp.concatenate([x, x - 0.25, y, y - 0.25], axis=0))
    cx, sx, cy, sy = [wave[k:k + 1] for k in range(4)]
    lines = [part[3 * a] + cy * part[3 * a + 1] + sy * part[3 * a + 2] for a in range(3)]
    vals = lines[0] + cx * lines[1] + sx * lines[2]
    p11, p12, p22 = vals[2:3], vals[3:4], vals[4:5]
    top, low = pos[2:4], pos[4:6]
    turn = jnp.concatenate([vals[0:2], p11 * top + p12 * low, p12 * top + p22 * low], axis=0)
    vel = vel - turn
    return pos + 0.5 * vel, vel


def kernel(
    n_los, tiles, hops, halves,
    state_hbm, defl_hbm, shear_hbm, routes_hbm, patches_hbm, reduce_hbm, out_hbm,
    state_ref, defl_ref, shear_ref, routes_ref, patches_ref, reduce_ref,
    gathered, tables, looked, outgoing, landed,
    load_sem, send_sem, recv_sem, pass_sem, move_sem, land_sem, store_sem,
):
    los, sky = lax.axis_index("los"), lax.axis_index("sky")
    rays, cells = state_ref.shape[1], defl_ref.shape[3]
    part_rays = rays // halves
    pair = sky + 1 - 2 * lax.rem(sky, 2)
    peers = [lax.rem(sky + 2 * step, tiles) for step in range(1, tiles // 2)]
    mates = [pair] + [lax.rem(pair + 2 * step, tiles) for step in range(1, tiles // 2)]
    after, before = lax.rem(los + 1, n_los), lax.rem(los + n_los - 1, n_los)

    barrier = pltpu.get_barrier_semaphore()
    friends = [(los, peer) for peer in peers] + [(los, pair), (after, sky), (before, sky)]
    for friend in friends:
        pl.semaphore_signal(barrier, inc=1, device_id=friend, device_id_type=MESH)

    pairs = [
        (reduce_hbm, reduce_ref), (defl_hbm, defl_ref), (shear_hbm, shear_ref),
        (patches_hbm, patches_ref), (routes_hbm, routes_ref), (state_hbm, state_ref),
    ]
    loads = [pltpu.make_async_copy(src, dst, load_sem.at[k]) for k, (src, dst) in enumerate(pairs)]
    for load in loads:
        load.start()
    for load in loads[:3]:
        load.wait()

    def sending(plane, tile, to, sent):
        return pltpu.make_async_remote_copy(
            src_ref=gathered.at[plane, tile], dst_ref=gathered.at[plane, tile],
            send_sem=sent, recv_sem=recv_sem.at[plane, tile],
            device_id=(los, to), device_id_type=MESH,
        )

    started = []
    cut = defl_ref.shape[2]
    lower = jnp.concatenate(pieces(reduce_ref[...], 3), axis=0)
    for plane in range(2):
        found = jnp.dot(lower[:, :cut], defl_ref[0, plane], preferred_element_type=jnp.float32)
        found += jnp.dot(lower[:, cut:], shear_ref[0, plane], preferred_element_type=jnp.float32)
        found = found[:HELD] + (found[HELD:2 * HELD] + found[2 * HELD:])
        gathered[plane, sky] = found[:SENT]
        if plane == 0:
            pl.semaphore_wait(barrier, len(friends))
        for step, to in enumerate([pair] + peers):
            if plane == 1:
                started[step].wait_send()
            copy = sending(plane, sky, to, send_sem.at[plane, step])
            copy.start()
            started.append(copy)
    started = started[tiles // 2:]
    for load in loads[3:]:
        load.wait()

    half_tiles = tiles // 2
    own = lax.rem(sky, 2)

    def build(plane, tile, other):
        held = jnp.concatenate([gathered[plane, tile], jnp.zeros((HELD - SENT, cells), jnp.float32)], axis=0)
        high, low = pieces(held, 2)
        tables[plane, other, tile // 2, :, :cells] = high
        tables[plane, other, tile // 2, :, cells:] = low

    def from_peers(plane):
        for step, peer in enumerate(peers):
            sending(plane, peer, pair, pass_sem.at[plane, step]).wait_recv()
            sending(plane, peer, pair, pass_sem.at[plane, step]).start()
        build(plane, sky, 0)
        for peer in peers:
            build(plane, peer, 0)

    def from_pair(plane):
        for mate in mates:
            sending(plane, mate, pair, pass_sem.at[plane, 0]).wait_recv()
            build(plane, mate, 1)

    group = min(half_tiles, 8)

    block = rays

    def lookup(hop, plane, others=(0, 1)):
        lanes = slice(None)
        both = patches_ref[hop, :, lanes]
        patch = jnp.where(plane == 0, both[0:1], both[1:2])
        route = jnp.broadcast_to(routes_ref[2 * hop + plane, :, lanes], (8, block))
        place = lax.broadcasted_iota(jnp.int32, (cells, block), 0)
        onehot = jnp.where(place == patch, 1.0, 0.0).astype(jnp.bfloat16)
        onehot = jnp.concatenate([onehot, onehot], axis=0)
        chosen = None
        if others[0] != 0:
            chosen = looked[hop, plane, :, lanes].reshape(HELD // 8, 8, block)
        for other in others:
            core = own if other == 0 else 1 - own
            for first in range(0, half_tiles, group):
                rows = tables[plane, other, first:first + group].reshape(group * HELD, 2 * cells)
                raw = jnp.dot(rows, onehot, preferred_element_type=jnp.float32)
                raw = raw.reshape(group, HELD // 8, 8, block)
                for k in range(group):
                    named = jnp.broadcast_to(route[None], raw[k].shape) == 2 * (first + k) + core
                    chosen = raw[k] if chosen is None else jnp.where(named, raw[k], chosen)
        looked[hop, plane, :, lanes] = chosen.reshape(HELD, block)

    def moved(hop, half):
        return pltpu.make_async_remote_copy(
            src_ref=outgoing.at[hop, half], dst_ref=landed.at[hop, half],
            send_sem=move_sem.at[hop, half], recv_sem=land_sem.at[hop, half],
            device_id=(after, sky), device_id_type=MESH,
        )

    def step_plane(hop, plane, half, pos, vel):
        lanes = slice(half * part_rays, (half + 1) * part_rays)
        part = [looked[hop, plane, ab * COMPS:ab * COMPS + 8, lanes] for ab in range(BASIS)]
        return advance(pos, vel, part)

    def parted(state):
        return (
            jnp.concatenate([state[0:2], state[4:8]], axis=0),
            jnp.concatenate([state[2:4], state[8:12]], axis=0),
        )

    def send_on(hop, half, pos, vel):
        outgoing[hop, half, 0:2] = pos[0:2]
        outgoing[hop, half, 2:4] = vel[0:2]
        outgoing[hop, half, 4:8] = pos[2:6]
        outgoing[hop, half, 8:12] = vel[2:6]
        moved(hop, half).start()

    def first_hop(plane, rays_now):
        from_peers(plane)
        lookup(0, plane, (0,))
        from_pair(plane)
        lookup(0, plane, (1,))
        return tuple(step_plane(0, plane, half, *rays_now[half]) for half in range(halves))

    at_start = tuple(
        parted(state_ref[:, half * part_rays:(half + 1) * part_rays]) for half in range(halves)
    )
    after_first = lax.fori_loop(0, 2, first_hop, at_start)
    for half in range(halves):
        send_on(0, half, *after_first[half])

    def later_hop(hop, carry):
        def both_planes(plane, inner):
            lookup(hop, plane)
            return inner

        lax.fori_loop(0, 2, both_planes, 0)
        for half in range(halves):
            moved(hop - 1, half).wait_recv()
            rays_now = parted(landed[hop - 1, half])
            for plane in range(2):
                rays_now = step_plane(hop, plane, half, *rays_now)
            send_on(hop, half, *rays_now)
        return carry

    lax.fori_loop(1, hops, later_hop, 0)
    stores = []
    for half in range(halves):
        moved(hops - 1, half).wait_recv()
        lanes = pl.ds(half * part_rays, part_rays)
        store = pltpu.make_async_copy(landed.at[hops - 1, half], out_hbm.at[:, lanes], store_sem.at[half])
        store.start()
        stores.append(store)
    for copy in started:
        copy.wait_send()
    for plane in range(2):
        for step, peer in enumerate(peers):
            sending(plane, peer, pair, pass_sem.at[plane, step]).wait_send()
    for hop in range(hops):
        for half in range(halves):
            moved(hop, half).wait_send()
    for store in stores:
        store.wait()


def body(n_los, tiles, state, deflection, shear, routes, patches):
    hops, rays, cells = routes.shape[0], state.shape[1], deflection.shape[3]
    halves = 2
    routes = routes.reshape(hops * 2, 1, rays)
    inputs = (state, deflection, shear, routes, patches, jnp.asarray(reduction()))
    return pl.pallas_call(
        functools.partial(kernel, n_los, tiles, hops, halves),
        out_shape=jax.ShapeDtypeStruct(state.shape, jnp.float32),
        in_specs=[pl.BlockSpec(memory_space=pltpu.HBM)] * 6,
        out_specs=pl.BlockSpec(memory_space=pltpu.HBM),
        scratch_shapes=[pltpu.VMEM(array.shape, array.dtype) for array in inputs] + [
            pltpu.VMEM((2, tiles, SENT, cells), jnp.float32),
            pltpu.VMEM((2, 2, tiles // 2, HELD, 2 * cells), jnp.bfloat16),
            pltpu.VMEM((hops, 2, HELD, rays), jnp.float32),
            pltpu.VMEM((hops, halves, state.shape[0], rays // halves), jnp.float32),
            pltpu.VMEM((hops, halves, state.shape[0], rays // halves), jnp.float32),
            pltpu.SemaphoreType.DMA((len(inputs),)),
            pltpu.SemaphoreType.DMA((2, tiles // 2)),
            pltpu.SemaphoreType.DMA((2, tiles)),
            pltpu.SemaphoreType.DMA((2, tiles // 2)),
            pltpu.SemaphoreType.DMA((hops, halves)),
            pltpu.SemaphoreType.DMA((hops, halves)),
            pltpu.SemaphoreType.DMA((halves,)),
        ],
        compiler_params=pltpu.CompilerParams(
            collective_id=0, has_side_effects=True, vmem_limit_bytes=64 * 2**20
        ),
    )(*inputs)


def solution(mesh):
    placed = (
        P(None, ("los", "sky")),
        P("los", None, None, "sky"),
        P("los", None, None, "sky"),
        P(None, None, ("los", "sky"), None),
        P(None, None, ("los", "sky")),
    )
    return jax.shard_map(
        functools.partial(body, mesh.shape["los"], mesh.shape["sky"]),
        mesh=mesh, in_specs=placed, out_specs=P(None, ("los", "sky")), check_vma=False,
    )
```
